32 devices in a mesh: seq: 4 (over y, x), head: 8 (over z, core).
Axes of the slice: x: 2, y: 2, z: 4, core: 2. Of those that a mesh axis runs over, the one named last changes fastest.
Arguments:
- tokens: bfloat16 [2, 4096, 4096], P(None, 'seq', 'head'), may hold values from -6 to 6
- w_gate: bfloat16 [4096, 2048], P(None, 'head'), may hold values from -0.09375 to 0.09375
- w_value: bfloat16 [4096, 2048], P(None, 'head'), may hold values from -0.09375 to 0.09375
- w_bc: bfloat16 [4096, 256], replicated, may hold values from -0.09375 to 0.09375
- w_step: bfloat16 [4096, 32], P(None, 'head'), may hold values from -0.09375 to 0.09375
- step_bias: float32 [32], P('head'), may hold values from -1 to 1
- rate: float32 [32], P('head'), may hold values from 1.2207031e-05 to 0.1
- conv_value: float32 [4, 2048], P(None, 'head'), may hold values from -3 to 3
- conv_bc: float32 [4, 256], replicated, may hold values from -3 to 3
- norm_gain: float32 [2048], P('head'), may hold values from 0.5 to 1.5
- w_out: bfloat16 [2048, 4096], P('head'), may hold values from -0.1875 to 0.1875
- kept_states: float32 [32, 32, 64, 128], P('seq', 'head'), may hold values from -2.4 to 2.4
- kept_index: int32 [2], replicated, may hold values from 0 to 31
- cached_len: int32 [2], replicated, may hold values from 0 to 4095
Outputs:
- mixed: bfloat16 [2, 4096, 4096], P(None, 'seq', 'head')
The draws below stay inside these ranges and needn't reach their ends.
Inputs may be any that keep to these rules, and one draw needn't show every extreme that they name: Prompt b starts from kept state kept_index[b]; positions below cached_len[b] are already folded into that state.
All inputs are finite; a program needn't handle non-finite values.
Results may differ from the reference program's by a relative error of at most 0.028.
Values may be sent and summed in bfloat16 or wider, within the bound.
A program may use at most 128 MiB of HBM per device.

```python
import math
import jax
import jax.numpy as jnp
from jax import lax

D = 4096
HEAD_SIZE = 64
STATE = 128
CONV = 4
BATCH = 2
HEADS = 32
INNER = 2048
LEN = 4096
POOL = 32
N_HEAD = 8


def strengthened(entries, stream_key, source, target, shards_of, factor):
    def block_of(axis_at):
        return (jnp.arange(entries.shape[axis_at]) // (entries.shape[axis_at] // shards_of)).reshape((-1,) + (1,) * (entries.ndim - 1 - axis_at))

    near = jax.random.permutation(stream_key, shards_of)[block_of(target)]
    other_side = (block_of(target) + shards_of // 2) % shards_of
    return jnp.where((block_of(source) == near) | (block_of(source) == other_side), factor * entries, entries)


def level_of(rng, shape, split, low, high):
    loudness = 1.0
    for axis_at, shards_of in split:
        draws = jax.random.uniform(jax.random.fold_in(jax.random.fold_in(rng, 6), axis_at), (shards_of,), jnp.float32, low / len(split), high / len(split))
        loudness = loudness * jnp.repeat(jnp.exp(draws), shape[axis_at] // shards_of).reshape((-1,) + (1,) * (len(shape) - 1 - axis_at))
    return loudness


def normal_values(stream_key, extent, deviation, reach, shards=(), held_as=jnp.bfloat16):
    gain = level_of(stream_key, extent, shards, -0.22, 0.18) if shards else 1.0
    result = jax.random.normal(stream_key, extent, jnp.float32) * deviation * gain
    return jnp.minimum(jnp.maximum(result, -reach), reach).astype(held_as)


def gaussian_with(key, shape, spread, limit, cuts, heavy, kind=jnp.bfloat16):
    result = spread * jax.random.normal(key, shape, jnp.float32)
    if cuts:
        result = result * level_of(key, shape, cuts, -0.22, 0.18)
    return jnp.clip(strengthened(result, jax.random.fold_in(key, 3), *heavy), -limit, limit).astype(kind)


def setup_inputs(seed: int = 0) -> dict:
    key_list = jax.random.split(jax.random.key(seed), 15)
    return {
        "tokens": normal_values(key_list[0], (BATCH, LEN, D), 1.0, 6.0, ((1, 4), (2, 8))),
        "w_gate": normal_values(key_list[1], (D, INNER), D ** -0.5, 0.09375, ((1, 8),)),
        "w_value": normal_values(key_list[2], (D, INNER), D ** -0.5, 0.09375, ((1, 8),)),
        "w_bc": normal_values(key_list[3], (D, 2 * STATE), D ** -0.5, 0.09375),
        "w_step": normal_values(key_list[4], (D, HEADS), D ** -0.5, 0.09375, ((1, 8),)),
        "step_bias": jnp.clip(jax.random.uniform(key_list[5], (HEADS,), jnp.float32, -1.0, 1.0) * level_of(key_list[5], (HEADS,), ((0, 8),), -0.4, 0.0), -1.0, 1.0),
        "rate": jnp.clip(jnp.exp(math.log(0.1) - 9.010913 * jax.random.uniform(key_list[6], (HEADS,), jnp.float32) ** level_of(key_list[6], (HEADS,), ((0, 8),), -0.2, 0.2)), 1.220703143189894e-05, 0.1),
        "conv_value": normal_values(key_list[7], (CONV, INNER), CONV ** -0.5, 3.0, ((1, 8),), jnp.float32),
        "conv_bc": normal_values(key_list[8], (CONV, 2 * STATE), CONV ** -0.5, 3.0, (), jnp.float32),
        "norm_gain": jnp.clip(1.0 + 0.1 * jax.random.normal(key_list[9], (INNER,), jnp.float32), 0.5, 1.5),
        "w_out": gaussian_with(key_list[10], (INNER, D), INNER ** -0.5, 0.1875, ((0, 8),), (0, 1, 8, 2.0)),
        "kept_states": normal_values(key_list[11], (POOL, HEADS, HEAD_SIZE, STATE), 0.3, 2.4, ((0, 4), (1, 8)), jnp.float32),
        "kept_index": jax.random.randint(key_list[12], (BATCH,), 0, POOL).astype(jnp.int32),
        "cached_len": jax.random.randint(key_list[13], (BATCH,), 0, LEN).astype(jnp.int32),
    }


def scan_step(state, inputs):
    dec, drive, bvec, cvec = inputs
    state = dec[:, :, None, None] * state + drive[:, :, :, None] * bvec[:, None, None, :]
    out = jnp.einsum('bhpn,bn->bhp', state, cvec, precision=lax.Precision.HIGHEST)
    return (state, out)

def add_partial(total, pieces):
    rows, weights = pieces
    part = jnp.dot(rows, weights, preferred_element_type=jnp.float32).astype(jnp.bfloat16)
    part = lax.optimization_barrier(part)
    return (total + part.astype(jnp.float32), None)

def reference(tokens, w_gate, w_value, w_bc, w_step, step_bias, rate, conv_value, conv_bc, norm_gain, w_out, kept_states, kept_index, cached_len):
    flat = tokens.reshape(BATCH * LEN, D)
    gate = jnp.dot(flat, w_gate, preferred_element_type=jnp.float32).astype(jnp.bfloat16)
    value = jnp.dot(flat, w_value, preferred_element_type=jnp.float32).astype(jnp.bfloat16)
    bc_part = jnp.dot(flat, w_bc, preferred_element_type=jnp.float32).astype(jnp.bfloat16)
    step_raw = jnp.dot(flat, w_step, preferred_element_type=jnp.float32).astype(jnp.bfloat16)
    mixin = jnp.concatenate([value, bc_part], axis=1).astype(jnp.float32).reshape(BATCH, LEN, -1)
    taps = jnp.concatenate([conv_value, conv_bc], axis=1)
    padded = jnp.pad(mixin, ((0, 0), (CONV - 1, 0), (0, 0)))
    conv = jnp.zeros_like(mixin)
    for k in range(CONV):
        conv = conv + taps[k][None, None, :] * padded[:, k:k + LEN, :]
    conv = jax.nn.silu(conv)
    xs = conv[:, :, :INNER].reshape(BATCH, LEN, HEADS, HEAD_SIZE)
    bmat = conv[:, :, INNER:INNER + STATE]
    cmat = conv[:, :, INNER + STATE:]
    positions = jnp.arange(LEN, dtype=jnp.int32)
    mask = (positions[None, :] >= cached_len[:, None]).astype(jnp.float32)
    dt = jax.nn.softplus(step_raw.astype(jnp.float32).reshape(BATCH, LEN, HEADS) + step_bias[None, None, :]) * mask[:, :, None]
    decay = jnp.exp(-dt * rate[None, None, :])
    drive = dt[:, :, :, None] * xs
    start = kept_states[kept_index.astype(jnp.int32)]
    inputs = (decay.transpose(1, 0, 2), drive.transpose(1, 0, 2, 3), bmat.transpose(1, 0, 2), cmat.transpose(1, 0, 2))
    final, ys = lax.scan(scan_step, start, inputs)
    y = ys.transpose(1, 0, 2, 3)
    y = (y * mask[:, :, None, None]).reshape(BATCH * LEN, INNER)
    gated = y * jax.nn.silu(gate.astype(jnp.float32))
    meansq = lax.optimization_barrier(jnp.mean(gated * gated, axis=1, keepdims=True))
    normed = (gated * lax.rsqrt(meansq + 1e-05) * norm_gain[None, :]).astype(jnp.bfloat16)
    block = INNER // N_HEAD
    row_blocks = normed.reshape(BATCH * LEN, N_HEAD, block).transpose(1, 0, 2)
    weight_blocks = w_out.reshape(N_HEAD, block, D)
    summed, unused = lax.scan(add_partial, jnp.zeros((BATCH * LEN, D), jnp.float32), (row_blocks, weight_blocks))
    return summed.astype(jnp.bfloat16).reshape(BATCH, LEN, D)
```

```python
import functools

import jax
import jax.numpy as jnp
from jax import lax
from jax.experimental import pallas as pl
from jax.experimental.pallas import tpu as pltpu
from jax.sharding import PartitionSpec as P

CONV = 4
LANES = 128
CHUNK = 128
F32 = jnp.float32
BF16 = jnp.bfloat16


def silu(x):
    return x * (1.0 / (1.0 + jnp.exp(-x)))


def softplus(x):
    return jnp.maximum(x, 0.0) + jnp.log1p(jnp.exp(-jnp.abs(x)))


def per_head(cols, heads, size):
    rows = cols.shape[0]
    return jnp.concatenate(
        [jnp.broadcast_to(cols[:, h : h + 1], (rows, size)) for h in range(heads)], axis=1
    )


def scan_kernel(
    heads, inner, state, mixin_ref, step_ref, before_ref, taps_ref, bias_ref, rate_ref, start_ref,
    y_ref, c_ref, grow_ref, sec_ref, total_ref, tail, held, passed,
):
    i = pl.program_id(0)
    rows = mixin_ref.shape[0]
    size = inner // heads

    @pl.when(i == 0)
    def _():
        tail[...] = before_ref[...].astype(F32)
        held[...] = jnp.zeros_like(held)
        passed[...] = jnp.zeros_like(passed)

    mixin = mixin_ref[...].astype(F32)
    padded = jnp.concatenate([tail[...], mixin], axis=0)
    tail[...] = mixin[rows - 8 :, :]
    conv = taps_ref[0:1, :] * padded[8 - CONV + 1 : 8 - CONV + 1 + rows, :]
    for k in range(1, CONV):
        conv = conv + taps_ref[k : k + 1, :] * padded[8 - CONV + 1 + k : 8 - CONV + 1 + k + rows, :]
    conv = silu(conv)
    xs = conv[:, :inner]
    bmat = conv[:, inner : inner + state].astype(BF16)
    cmat = conv[:, inner + state :].astype(BF16)
    c_ref[...] = cmat
    line = lax.broadcasted_iota(jnp.int32, (rows, LANES), 0)
    dt = softplus(step_ref[...].astype(F32) + bias_ref[...])
    dt = jnp.where(line + i * rows >= start_ref[0], dt, 0.0)
    tri_r = lax.broadcasted_iota(jnp.int32, (rows, rows), 0)
    tri_c = lax.broadcasted_iota(jnp.int32, (rows, rows), 1)
    lower = tri_r >= tri_c
    cumul = jnp.dot(
        lower.astype(F32), -dt * rate_ref[...],
        precision=lax.Precision.HIGHEST, preferred_element_type=F32,
    )
    cumul_t = cumul.T
    last = cumul[rows - 1 : rows, :]
    scores = lax.dot_general(cmat, bmat, (((1,), (1,)), ((), ())), preferred_element_type=F32)
    scores = jnp.where(lower, scores, 0.0)
    drive = per_head(dt, heads, size) * xs
    drive16 = drive.astype(BF16)
    from_held = lax.dot_general(
        cmat, held[...].astype(BF16), (((1,), (1,)), ((), ())), preferred_element_type=F32
    )
    within = jnp.exp(cumul)
    y = per_head(within, heads, size) * from_held
    parts = []
    for h in range(heads):
        diff = cumul[:, h : h + 1] - cumul_t[h : h + 1, :]
        weighting = (jnp.exp(jnp.minimum(diff, 0.0)) * scores).astype(BF16)
        parts.append(
            jnp.dot(weighting, drive16[:, h * size : (h + 1) * size], preferred_element_type=F32)
        )
    y_ref[...] = y + jnp.concatenate(parts, axis=1)
    to_end = per_head(jnp.exp(last - cumul), heads, size)
    added = lax.dot_general(
        (to_end * drive).astype(BF16), bmat, (((0,), (0,)), ((), ())), preferred_element_type=F32
    )
    for h in range(heads):
        keep = jnp.exp(last[:, h : h + 1])
        at = slice(h * size, (h + 1) * size)
        held[at, :] = keep * held[at, :] + added[at, :]
    grow_ref[...] = jnp.exp(cumul + passed[0:1, :])
    passed[...] = passed[...] + last
    sec_ref[...] = held[...]
    total_ref[...] = jnp.exp(passed[...])


def scan_section(proj, before, taps, bias, rate, start, heads, inner, state):
    length = proj.shape[0]
    mix = inner + 2 * state
    step_at = (mix + inner) // LANES
    whole = lambda shape: pl.BlockSpec(shape, lambda i: (0,) * len(shape))
    return pl.pallas_call(
        functools.partial(scan_kernel, heads, inner, state),
        grid=(length // CHUNK,),
        in_specs=[
            pl.BlockSpec((CHUNK, mix), lambda i: (i, 0)),
            pl.BlockSpec((CHUNK, LANES), lambda i: (i, step_at)),
            whole((8, mix)),
            whole((CONV, mix)),
            whole((1, LANES)),
            whole((1, LANES)),
            pl.BlockSpec(memory_space=pltpu.SMEM),
        ],
        out_specs=[
            pl.BlockSpec((CHUNK, inner), lambda i: (i, 0)),
            pl.BlockSpec((CHUNK, state), lambda i: (i, 0)),
            pl.BlockSpec((CHUNK, LANES), lambda i: (i, 0)),
            whole((inner, state)),
            whole((8, LANES)),
        ],
        out_shape=[
            jax.ShapeDtypeStruct((length, inner), F32),
            jax.ShapeDtypeStruct((length, state), BF16),
            jax.ShapeDtypeStruct((length, LANES), F32),
            jax.ShapeDtypeStruct((inner, state), F32),
            jax.ShapeDtypeStruct((8, LANES), F32),
        ],
        scratch_shapes=[
            pltpu.VMEM((8, mix), F32),
            pltpu.VMEM((inner, state), F32),
            pltpu.VMEM((8, LANES), F32),
        ],
        cost_estimate=pl.CostEstimate(
            flops=2 * length * inner * 4 * LANES, bytes_accessed=length * 4096,
            transcendentals=length * 2048,
        ),
        name="section_scan",
    )(proj, proj, before, taps, bias, rate, start)


def gate_kernel(heads, y_ref, c_ref, grow_ref, gate_ref, inc_ref, gain_ref, start_ref, g_ref, sq_ref):
    i = pl.program_id(0)
    rows, inner = y_ref.shape
    carry = lax.dot_general(
        c_ref[...], inc_ref[...], (((1,), (1,)), ((), ())), preferred_element_type=F32
    )
    y = y_ref[...] + per_head(grow_ref[...], heads, inner // heads) * carry
    line = lax.broadcasted_iota(jnp.int32, (rows, inner), 0)
    y = jnp.where(line + i * rows >= start_ref[0], y, 0.0)
    gated = y * silu(gate_ref[...].astype(F32))
    sq_ref[...] = jnp.broadcast_to(jnp.sum(gated * gated, axis=1, keepdims=True), sq_ref.shape)
    g_ref[...] = (gated * gain_ref[...]).astype(BF16)


def gate_section(y, cmat, grow, proj, incoming, gain, start, heads, mix):
    length, inner = y.shape
    state = cmat.shape[1]
    rows = 256
    at = mix // inner
    return pl.pallas_call(
        functools.partial(gate_kernel, heads),
        grid=(length // rows,),
        in_specs=[
            pl.BlockSpec((rows, inner), lambda i: (i, 0)),
            pl.BlockSpec((rows, state), lambda i: (i, 0)),
            pl.BlockSpec((rows, LANES), lambda i: (i, 0)),
            pl.BlockSpec((rows, inner), lambda i: (i, at)),
            pl.BlockSpec((inner, state), lambda i: (0, 0)),
            pl.BlockSpec((1, inner), lambda i: (0, 0)),
            pl.BlockSpec(memory_space=pltpu.SMEM),
        ],
        out_specs=[
            pl.BlockSpec((rows, inner), lambda i: (i, 0)),
            pl.BlockSpec((rows, LANES), lambda i: (i, 0)),
        ],
        out_shape=[
            jax.ShapeDtypeStruct((length, inner), BF16),
            jax.ShapeDtypeStruct((length, LANES), F32),
        ],
        cost_estimate=pl.CostEstimate(
            flops=2 * length * inner * LANES, bytes_accessed=length * 3000,
            transcendentals=length * inner,
        ),
        name="section_gate",
    )(y, cmat, grow, proj, incoming, gain, start)


def high_low(x):
    high = x.astype(BF16)
    return high, (x - high.astype(F32)).astype(BF16)


def per_device(
    tokens, w_gate, w_value, w_bc, w_step, step_bias, rate, conv_value, conv_bc, norm_gain,
    w_out, kept_states, kept_index, cached_len,
):
    batch, sec_len, d_part = tokens.shape
    inner = w_gate.shape[1]
    heads = w_step.shape[1]
    size = inner // heads
    state = w_bc.shape[1] // 2
    mix = inner + 2 * state
    slots = kept_states.shape[0]
    n_seq = lax.axis_size("seq")
    n_head = lax.axis_size("head")
    sec = lax.axis_index("seq")

    pieces = [lax.all_gather(tokens[b], "head", axis=1, tiled=True) for b in range(batch)]
    w_cols = lax.all_to_all(w_out, "head", split_axis=1, concat_axis=0, tiled=True)
    weights = jnp.concatenate(
        [w_value, w_bc, w_gate, jnp.pad(w_step, ((0, 0), (0, LANES - heads)))], axis=1
    )
    taps = jnp.concatenate([conv_value, conv_bc], axis=1)
    bias = jnp.pad(step_bias, (0, LANES - heads))[None]
    rates = jnp.pad(rate, (0, LANES - heads))[None]
    gain = norm_gain[None]
    picked = jnp.stack(
        [lax.dynamic_index_in_dim(kept_states, kept_index[b] % slots, 0, False) for b in range(batch)]
    ).astype(BF16).reshape(batch, inner, state)
    kept = lax.all_gather(picked, "seq", axis=0)

    outs = []
    for b in range(batch):
        proj = jnp.dot(pieces[b], weights, preferred_element_type=F32).astype(BF16)
        before = lax.ppermute(
            proj[sec_len - 8 :, :mix], "seq", [(i, i + 1) for i in range(n_seq - 1)]
        )
        start = (cached_len[b] - sec * sec_len)[None]
        y, cmat, grow, sec_state, total = scan_section(
            proj, before, taps, bias, rates, start, heads, inner, state
        )
        high, low = high_low(total)
        sent = jnp.concatenate([sec_state.astype(BF16), high, low], axis=0)
        got = lax.all_gather(sent, "seq", axis=0)
        incoming = lax.dynamic_index_in_dim(kept, kept_index[b] // slots, 0, False)[b]
        incoming = incoming.astype(F32).reshape(heads, size, state)
        for r in range(n_seq - 1):
            decay = got[r, inner, :heads].astype(F32) + got[r, inner + 8, :heads].astype(F32)
            later = decay[:, None, None] * incoming + got[r, :inner].astype(F32).reshape(
                heads, size, state
            )
            incoming = jnp.where(r < sec, later, incoming)
        g, squares = gate_section(
            y, cmat, grow, proj, incoming.reshape(inner, state).astype(BF16), gain, start, heads, mix
        )
        g_all = lax.all_gather(g, "head", axis=1, tiled=True)
        sq_all = lax.all_gather(squares[:, 0], "head", axis=0)
        meansq = jnp.sum(sq_all, axis=0) / (inner * n_head)
        mixed = jnp.dot(g_all, w_cols, preferred_element_type=F32)
        outs.append((mixed * lax.rsqrt(meansq + 1e-05)[:, None]).astype(BF16))
    return jnp.stack(outs)


def solution(mesh):
    return jax.shard_map(
        per_device,
        mesh=mesh,
        in_specs=(
            P(None, "seq", "head"),
            P(None, "head"),
            P(None, "head"),
            P(),
            P(None, "head"),
            P("head"),
            P("head"),
            P(None, "head"),
            P(),
            P("head"),
            P("head", None),
            P("seq", "head", None, None),
            P(),
            P(),
        ),
        out_specs=P(None, "seq", "head"),
        check_vma=False,
    )
```

```python
import functools

import jax
import jax.numpy as jnp
from jax import lax
from jax.experimental import pallas as pl
from jax.experimental.pallas import tpu as pltpu
from jax.sharding import PartitionSpec as P

CONV = 4
LANES = 128
CHUNK = 128
F32 = jnp.float32
BF16 = jnp.bfloat16


def silu(x):
    return x * (1.0 / (1.0 + jnp.exp(-x)))


def softplus(x):
    return jnp.maximum(x, 0.0) + jnp.log1p(jnp.exp(-jnp.abs(x)))


def per_head(cols, heads, size):
    rows = cols.shape[0]
    return jnp.concatenate(
        [jnp.broadcast_to(cols[:, h : h + 1], (rows, size)) for h in range(heads)], axis=1
    )


def scan_kernel(
    heads, inner, state, mixin_ref, step_ref, before_ref, taps_ref, bias_ref, rate_ref, start_ref,
    y_ref, c_ref, grow_ref, sec_ref, total_ref, tail, held, passed,
):
    i = pl.program_id(0)
    batch, rows = mixin_ref.shape[:2]
    size = inner // heads

    @pl.when(i == 0)
    def _():
        tail[...] = before_ref[...].astype(F32)
        held[...] = jnp.zeros_like(held)
        passed[...] = jnp.zeros_like(passed)

    tri_r = lax.broadcasted_iota(jnp.int32, (rows, rows), 0)
    tri_c = lax.broadcasted_iota(jnp.int32, (rows, rows), 1)
    lower = tri_r >= tri_c
    line = lax.broadcasted_iota(jnp.int32, (rows, LANES), 0) + i * rows
    for b in range(batch):
        mixin = mixin_ref[b].astype(F32)
        padded = jnp.concatenate([tail[b], mixin], axis=0)
        tail[b] = mixin[rows - 8 :, :]
        first = 8 - CONV + 1
        conv = taps_ref[0:1, :] * padded[first : first + rows, :]
        for k in range(1, CONV):
            conv = conv + taps_ref[k : k + 1, :] * padded[first + k : first + k + rows, :]
        conv = silu(conv)
        xs = conv[:, :inner]
        bmat = conv[:, inner : inner + state].astype(BF16)
        cmat = conv[:, inner + state :].astype(BF16)
        c_ref[b] = cmat
        dt = softplus(step_ref[b].astype(F32) + bias_ref[...])
        dt = jnp.where(line >= start_ref[b], dt, 0.0)
        cumul = jnp.dot(
            lower.astype(F32), -dt * rate_ref[...],
            precision=lax.Precision.HIGHEST, preferred_element_type=F32,
        )
        cumul_t = cumul.T
        last = cumul[rows - 1 : rows, :]
        scores = lax.dot_general(cmat, bmat, (((1,), (1,)), ((), ())), preferred_element_type=F32)
        scores = jnp.where(lower, scores, 0.0)
        drive = per_head(dt, heads, size) * xs
        drive16 = drive.astype(BF16)
        from_held = lax.dot_general(
            cmat, held[b].astype(BF16), (((1,), (1,)), ((), ())), preferred_element_type=F32
        )
        y = per_head(jnp.exp(cumul), heads, size) * from_held
        parts = []
        for h in range(heads):
            diff = cumul[:, h : h + 1] - cumul_t[h : h + 1, :]
            weighting = (jnp.exp(jnp.minimum(diff, 0.0)) * scores).astype(BF16)
            parts.append(
                jnp.dot(
                    weighting, drive16[:, h * size : (h + 1) * size], preferred_element_type=F32
                )
            )
        y_ref[b] = y + jnp.concatenate(parts, axis=1)
        to_end = per_head(jnp.exp(last - cumul), heads, size)
        added = lax.dot_general(
            (to_end * drive).astype(BF16), bmat, (((0,), (0,)), ((), ())),
            preferred_element_type=F32,
        )
        for h in range(heads):
            keep = jnp.exp(last[:, h : h + 1])
            at = slice(h * size, (h + 1) * size)
            held[b, at, :] = keep * held[b, at, :] + added[at, :]
        grow_ref[b] = jnp.exp(cumul + passed[b, 0:1, :])
        passed[b] = passed[b] + last
    sec_ref[...] = held[...]
    total_ref[...] = jnp.exp(passed[...])


def scan_section(proj, before, taps, bias, rate, start, heads, inner, state):
    batch, length = proj.shape[:2]
    mix = inner + 2 * state
    step_at = (mix + inner) // LANES
    whole = lambda shape: pl.BlockSpec(shape, lambda i: (0,) * len(shape))
    rows = lambda width, at=0: pl.BlockSpec((batch, CHUNK, width), lambda i: (0, i, at))
    return pl.pallas_call(
        functools.partial(scan_kernel, heads, inner, state),
        grid=(length // CHUNK,),
        in_specs=[
            rows(mix),
            rows(LANES, step_at),
            whole((batch, 8, mix)),
            whole((CONV, mix)),
            whole((1, LANES)),
            whole((1, LANES)),
            pl.BlockSpec(memory_space=pltpu.SMEM),
        ],
        out_specs=[
            rows(inner),
            rows(state),
            rows(LANES),
            whole((batch, inner, state)),
            whole((batch, 8, LANES)),
        ],
        out_shape=[
            jax.ShapeDtypeStruct((batch, length, inner), F32),
            jax.ShapeDtypeStruct((batch, length, state), BF16),
            jax.ShapeDtypeStruct((batch, length, LANES), F32),
            jax.ShapeDtypeStruct((batch, inner, state), F32),
            jax.ShapeDtypeStruct((batch, 8, LANES), F32),
        ],
        scratch_shapes=[
            pltpu.VMEM((batch, 8, mix), F32),
            pltpu.VMEM((batch, inner, state), F32),
            pltpu.VMEM((batch, 8, LANES), F32),
        ],
        cost_estimate=pl.CostEstimate(
            flops=2 * batch * length * inner * 4 * LANES, bytes_accessed=batch * length * 4096,
            transcendentals=batch * length * 2048,
        ),
        name="section_scan",
    )(proj, proj, before, taps, bias, rate, start)


def gate_kernel(heads, y_ref, c_ref, grow_ref, gate_ref, inc_ref, gain_ref, start_ref, g_ref, sq_ref):
    i = pl.program_id(0)
    batch, rows, inner = y_ref.shape
    line = lax.broadcasted_iota(jnp.int32, (rows, inner), 0) + i * rows
    for b in range(batch):
        carry = lax.dot_general(
            c_ref[b], inc_ref[b], (((1,), (1,)), ((), ())), preferred_element_type=F32
        )
        y = y_ref[b] + per_head(grow_ref[b], heads, inner // heads) * carry
        y = jnp.where(line >= start_ref[b], y, 0.0)
        gated = y * silu(gate_ref[b].astype(F32))
        sq_ref[b] = jnp.broadcast_to(jnp.sum(gated * gated, axis=1, keepdims=True), (rows, LANES))
        g_ref[b] = (gated * gain_ref[...]).astype(BF16)


def gate_section(y, cmat, grow, proj, incoming, gain, start, heads, mix):
    batch, length, inner = y.shape
    state = cmat.shape[2]
    rows = lambda width, at=0: pl.BlockSpec((batch, 2 * CHUNK, width), lambda i: (0, i, at))
    return pl.pallas_call(
        functools.partial(gate_kernel, heads),
        grid=(length // (2 * CHUNK),),
        in_specs=[
            rows(inner),
            rows(state),
            rows(LANES),
            rows(inner, mix // inner),
            pl.BlockSpec((batch, inner, state), lambda i: (0, 0, 0)),
            pl.BlockSpec((1, inner), lambda i: (0, 0)),
            pl.BlockSpec(memory_space=pltpu.SMEM),
        ],
        out_specs=[rows(inner), rows(LANES)],
        out_shape=[
            jax.ShapeDtypeStruct((batch, length, inner), BF16),
            jax.ShapeDtypeStruct((batch, length, LANES), F32),
        ],
        cost_estimate=pl.CostEstimate(
            flops=2 * batch * length * inner * LANES, bytes_accessed=batch * length * 3000,
            transcendentals=batch * length * inner,
        ),
        name="section_gate",
    )(y, cmat, grow, proj, incoming, gain, start)


def remote(src, dst, send_sem, recv_sem, axis, index):
    return pltpu.make_async_remote_copy(
        src_ref=src, dst_ref=dst, send_sem=send_sem, recv_sem=recv_sem,
        device_id={axis: index}, device_id_type=pl.DeviceIdType.MESH,
    )


def greet(axes):
    barrier = pltpu.get_barrier_semaphore()
    count = 0
    for axis in axes:
        n = lax.axis_size(axis)
        me = lax.axis_index(axis)
        for o in range(1, n):
            pl.semaphore_signal(
                barrier, inc=1, device_id={axis: lax.rem(me + o, n)},
                device_id_type=pl.DeviceIdType.MESH,
            )
        count += n - 1
    pl.semaphore_wait(barrier, count)


def line_gather(x_ref, got, sems, recv, use, pieces, between):
    left_sem, right_sem, side_sem = sems
    n = lax.axis_size("head")
    chips = n // 2
    me = lax.axis_index("head")
    chip, core = me // 2, me % 2
    other = chip * 2 + 1 - core
    rows = x_ref.shape[0] // pieces

    def at(j):
        return pl.ds(pl.multiple_of(j * rows, rows), rows)

    def passed_on(src, slot, j, sem, index):
        return remote(src, got.at[slot, at(j)], sem.at[slot, j], recv.at[slot, j], "head", index)

    def arrived(slot, j):
        passed_on(got.at[slot, at(j)], slot, j, side_sem, other).wait_recv()

    def on_right(src, slot, j):
        return passed_on(src, slot, j, right_sem, me + 2)

    def on_left(src, slot, j):
        return passed_on(src, slot, j, left_sem, me - 2)

    def on_side(src, slot, j):
        return passed_on(src, slot, j, side_sem, other)

    has_right, has_left = chip + 1 < chips, chip > 0

    @pl.loop(0, pieces)
    def _(j):
        @pl.when(has_right)
        def _():
            on_right(x_ref.at[at(j)], me, j).start()

        @pl.when(has_left)
        def _():
            on_left(x_ref.at[at(j)], me, j).start()

        on_side(x_ref.at[at(j)], me, j).start()

    between(0)

    @pl.loop(0, pieces)
    def _(j):
        use(x_ref[at(j), :], me, at(j))

    def from_side(d, j):
        def here(q):
            slot = q * 2 + 1 - core
            arrived(slot, j)
            use(got[slot, at(j), :], slot, at(j))

        @pl.when(chip - d >= 0)
        def _():
            here(chip - d)

        @pl.when((chip + d < chips) & (d > 0))
        def _():
            here(chip + d)

    def step(t):
        d, j = t // pieces + 1, t % pieces
        low, high = (chip - d) * 2 + core, (chip + d) * 2 + core

        @pl.when(chip - d >= 0)
        def _():
            arrived(low, j)
            block = got.at[low, at(j)]

            @pl.when(has_right)
            def _():
                on_right(block, low, j).start()

            on_side(block, low, j).start()

        @pl.when(chip + d < chips)
        def _():
            arrived(high, j)
            block = got.at[high, at(j)]

            @pl.when(has_left)
            def _():
                on_left(block, high, j).start()

            on_side(block, high, j).start()

        @pl.when(chip - d >= 0)
        def _():
            use(got[low, at(j), :], low, at(j))

        @pl.when(chip + d < chips)
        def _():
            use(got[high, at(j), :], high, at(j))

        from_side(d - 1, j)

    pl.loop(0, pieces)(step)
    between(1)
    pl.loop(pieces, (chips - 1) * pieces)(step)

    @pl.loop(0, pieces)
    def _(j):
        from_side(chips - 1, j)

    @pl.loop(0, chips * pieces)
    def _(t):
        q, j = t // pieces, t % pieces
        slot = q * 2 + core
        block = got.at[slot, at(j)]
        on_side(block, slot, j).wait_send()

        @pl.when(has_right & (q <= chip))
        def _():
            on_right(block, slot, j).wait_send()

        @pl.when(has_left & (q >= chip))
        def _():
            on_left(block, slot, j).wait_send()

    between(2)


def project_kernel(
    pieces, x_ref, w_ref, wo_ref, out_ref, cols_ref,
    got, total, left_sem, right_sem, side_sem, recv, out_send, out_recv, seq_send, seq_recv, own_sem,
):
    n, n_seq = lax.axis_size("head"), lax.axis_size("seq")
    me, sec = lax.axis_index("head"), lax.axis_index("seq")
    part, width = cols_ref.shape[2:]
    greet(("head", "seq"))

    def columns(to):
        return wo_ref.at[
            pl.ds(pl.multiple_of(sec * part, part), part), pl.ds(pl.multiple_of(to * width, width), width)
        ]

    def spread(o):
        to = lax.rem(me + o, n)
        return remote(columns(to), cols_ref.at[sec, me], out_send.at[o], out_recv.at[me], "head", to)

    def landed(o):
        frm = lax.rem(me + o, n)
        remote(
            columns(frm), cols_ref.at[sec, frm], out_send.at[o], out_recv.at[frm], "head", frm
        ).wait_recv()

    def shared(o):
        to = lax.rem(sec + o, n_seq)
        return remote(cols_ref.at[sec], cols_ref.at[sec], seq_send.at[o], seq_recv.at[sec], "seq", to)

    def got_share(o):
        frm = lax.rem(sec + o, n_seq)
        remote(
            cols_ref.at[frm], cols_ref.at[frm], seq_send.at[o], seq_recv.at[frm], "seq", frm
        ).wait_recv()

    def own_copy():
        return pltpu.make_async_copy(columns(me), cols_ref.at[sec, me], own_sem)

    def between(stage):
        if stage == 0:
            own_copy().start()
            pl.loop(1, n)(lambda o: spread(o).start())
        elif stage == 1:
            own_copy().wait()
            pl.loop(1, n)(landed)
            pl.loop(1, n_seq)(lambda o: shared(o).start())
        else:
            pl.loop(1, n)(lambda o: spread(o).wait_send())
            pl.loop(1, n_seq)(lambda o: shared(o).wait_send())
            pl.loop(1, n_seq)(got_share)

    total[...] = jnp.zeros_like(total)

    def use(block, slot, at):
        total[at, :] += jnp.dot(block, w_ref[slot], preferred_element_type=F32)

    line_gather(x_ref, got, (left_sem, right_sem, side_sem), recv, use, pieces, between)

    @pl.loop(0, pieces)
    def _(j):
        rows = x_ref.shape[0] // pieces
        at = pl.ds(pl.multiple_of(j * rows, rows), rows)
        out_ref[at, :] = total[at, :].astype(BF16)


def mix_kernel(
    pieces, x_ref, sq_ref, w_ref, out_ref, sums_ref,
    got, left_sem, right_sem, side_sem, recv, sq_send, sq_recv, own_sem,
):
    n = lax.axis_size("head")
    me = lax.axis_index("head")
    parts, _, part, width = w_ref.shape
    greet(("head",))

    def sums_to(o):
        to = lax.rem(me + o, n)
        return remote(sq_ref, sums_ref.at[me], sq_send.at[o], sq_recv.at[me], "head", to)

    def sums_from(o):
        frm = lax.rem(me + o, n)
        remote(sq_ref, sums_ref.at[frm], sq_send.at[o], sq_recv.at[frm], "head", frm).wait_recv()

    def own_copy():
        return pltpu.make_async_copy(sq_ref, sums_ref.at[me], own_sem)

    def between(stage):
        if stage == 0:
            own_copy().start()
            pl.loop(1, n)(lambda o: sums_to(o).start())
        elif stage == 2:
            own_copy().wait()
            pl.loop(1, n)(lambda o: sums_to(o).wait_send())
            pl.loop(1, n)(sums_from)

    out_ref[...] = jnp.zeros_like(out_ref)

    def use(block, slot, at):
        weights = w_ref[:, slot].reshape(parts * part, width)
        out_ref[at, :] += jnp.dot(block, weights, preferred_element_type=F32)

    line_gather(x_ref, got, (left_sem, right_sem, side_sem), recv, use, pieces, between)


VMEM_SPEC = pl.BlockSpec(memory_space=pltpu.VMEM)


def gather_scratch(n, rows, width, pieces):
    sem = pltpu.SemaphoreType.DMA((n, pieces))
    return [pltpu.VMEM((n, rows, width), BF16)], [sem, sem, sem, sem]


def gather_project(x, weights, w_out, pieces=8):
    rows, width = x.shape
    n, n_seq = lax.axis_size("head"), lax.axis_size("seq")
    wide = weights.shape[2]
    depth, model = w_out.shape
    slots, sems = gather_scratch(n, rows, width, pieces)
    dma = pltpu.SemaphoreType.DMA
    return pl.pallas_call(
        functools.partial(project_kernel, pieces),
        in_specs=[VMEM_SPEC] * 3,
        out_specs=[VMEM_SPEC] * 2,
        out_shape=[
            jax.ShapeDtypeStruct((rows, wide), BF16),
            jax.ShapeDtypeStruct((n_seq, n, depth // n_seq, model // n), BF16),
        ],
        scratch_shapes=slots
        + [pltpu.VMEM((rows, wide), F32)]
        + sems
        + [dma((n,)), dma((n,)), dma((n_seq,)), dma((n_seq,)), dma(())],
        compiler_params=pltpu.CompilerParams(
            collective_id=0, has_side_effects=True, vmem_limit_bytes=56 * 2**20
        ),
        name="gather_project",
    )(x, weights, w_out)


def gather_mix(g, squares, w_cols, pieces=8):
    rows, width = g.shape
    n = lax.axis_size("head")
    slots, sems = gather_scratch(n, rows, width, pieces)
    dma = pltpu.SemaphoreType.DMA
    return pl.pallas_call(
        functools.partial(mix_kernel, pieces),
        in_specs=[VMEM_SPEC] * 3,
        out_specs=[VMEM_SPEC] * 2,
        out_shape=[
            jax.ShapeDtypeStruct((rows, w_cols.shape[3]), F32),
            jax.ShapeDtypeStruct((n,) + squares.shape, F32),
        ],
        scratch_shapes=slots + sems + [dma((n,)), dma((n,)), dma(())],
        compiler_params=pltpu.CompilerParams(
            collective_id=1, has_side_effects=True, vmem_limit_bytes=48 * 2**20
        ),
        name="gather_mix",
    )(g, squares, w_cols)


def high_low(x):
    high = x.astype(BF16)
    return high, (x - high.astype(F32)).astype(BF16)


def per_device(
    tokens, w_gate, w_value, w_bc, w_step, step_bias, rate, conv_value, conv_bc, norm_gain,
    w_out, kept_states, kept_index, cached_len,
):
    batch, sec_len, d_part = tokens.shape
    inner = w_gate.shape[1]
    heads = w_step.shape[1]
    size = inner // heads
    state = w_bc.shape[1] // 2
    mix = inner + 2 * state
    slots = kept_states.shape[0]
    n_seq = lax.axis_size("seq")
    n_head = lax.axis_size("head")
    sec = lax.axis_index("seq")

    weights = jnp.concatenate(
        [w_value, w_bc, w_gate, jnp.pad(w_step, ((0, 0), (0, LANES - heads)))], axis=1
    ).reshape(n_head, d_part, -1)
    taps = jnp.concatenate([conv_value, conv_bc], axis=1)
    bias = jnp.pad(step_bias, (0, LANES - heads))[None]
    rates = jnp.pad(rate, (0, LANES - heads))[None]
    picked = jnp.stack(
        [lax.dynamic_index_in_dim(kept_states, kept_index[b] % slots, 0, False) for b in range(batch)]
    ).astype(BF16).reshape(batch, inner, state)
    start = cached_len - sec * sec_len

    proj, w_cols = gather_project(tokens.reshape(batch * sec_len, d_part), weights, w_out)
    proj = proj.reshape(batch, sec_len, -1)
    before = lax.ppermute(
        proj[:, sec_len - 8 :, :mix], "seq", [(i, i + 1) for i in range(n_seq - 1)]
    )
    y, cmat, grow, sec_state, total = scan_section(
        proj, before, taps, bias, rates, start, heads, inner, state
    )
    high, low = high_low(total)
    sent = jnp.concatenate([sec_state.astype(BF16), high, low, picked], axis=1)
    got = lax.all_gather(sent, "seq", axis=0)
    incoming = jnp.stack(
        [
            lax.dynamic_index_in_dim(got[:, b, inner + 16 :], kept_index[b] // slots, 0, False)
            for b in range(batch)
        ]
    )
    incoming = incoming.astype(F32).reshape(batch, heads, size, state)
    for r in range(n_seq - 1):
        decay = got[r, :, inner, :heads].astype(F32) + got[r, :, inner + 8, :heads].astype(F32)
        later = decay[:, :, None, None] * incoming + got[r, :, :inner].astype(F32).reshape(
            batch, heads, size, state
        )
        incoming = jnp.where(r < sec, later, incoming)
    g, squares = gate_section(
        y, cmat, grow, proj, incoming.reshape(batch, inner, state).astype(BF16),
        norm_gain[None], start, heads, mix,
    )
    mixed, sums = gather_mix(
        g.reshape(batch * sec_len, inner), squares[:, :, 0].reshape(-1, LANES), w_cols
    )
    meansq = jnp.sum(sums, axis=0).reshape(-1) / (inner * n_head)
    out = (mixed * lax.rsqrt(meansq + 1e-05)[:, None]).astype(BF16)
    return out.reshape(batch, sec_len, d_part)


def solution(mesh):
    return jax.shard_map(
        per_device,
        mesh=mesh,
        in_specs=(
            P(None, "seq", "head"),
            P(None, "head"),
            P(None, "head"),
            P(),
            P(None, "head"),
            P("head"),
            P("head"),
            P(None, "head"),
            P(),
            P("head"),
            P("head", None),
            P("seq", "head", None, None),
            P(),
            P(),
        ),
        out_specs=P(None, "seq", "head"),
        check_vma=False,
    )
```

```python
import functools

import jax
import jax.numpy as jnp
from jax import lax
from jax.experimental import pallas as pl
from jax.experimental.pallas import tpu as pltpu
from jax.sharding import PartitionSpec as P

CONV = 4
LANES = 128
CHUNK = 128
F32 = jnp.float32
BF16 = jnp.bfloat16


def silu(x):
    return x * (1.0 / (1.0 + jnp.exp(-x)))


def softplus(x):
    return jnp.maximum(x, 0.0) + jnp.log1p(jnp.exp(-jnp.abs(x)))


def per_head(cols, heads, size):
    rows = cols.shape[0]
    return jnp.concatenate(
        [jnp.broadcast_to(cols[:, h : h + 1], (rows, size)) for h in range(heads)], axis=1
    )


def scan_kernel(
    heads, inner, state, mixin_ref, step_ref, before_ref, taps_ref, bias_ref, rate_ref, start_ref,
    y_ref, c_ref, grow_ref, sec_ref, total_ref, tail, held, passed,
):
    i = pl.program_id(0)
    batch, rows = mixin_ref.shape[:2]
    size = inner // heads

    @pl.when(i == 0)
    def _():
        tail[...] = before_ref[:, 8:, :].astype(F32)
        held[...] = jnp.zeros_like(held)
        passed[...] = jnp.zeros_like(passed)

    tri_r = lax.broadcasted_iota(jnp.int32, (rows, rows), 0)
    tri_c = lax.broadcasted_iota(jnp.int32, (rows, rows), 1)
    lower = tri_r >= tri_c
    line = lax.broadcasted_iota(jnp.int32, (rows, LANES), 0) + i * rows
    for b in range(batch):
        mixin = mixin_ref[b].astype(F32)
        padded = jnp.concatenate([tail[b], mixin], axis=0)
        tail[b] = mixin[rows - 8 :, :]
        first = 8 - CONV + 1
        conv = taps_ref[0:1, :] * padded[first : first + rows, :]
        for k in range(1, CONV):
            conv = conv + taps_ref[k : k + 1, :] * padded[first + k : first + k + rows, :]
        conv = silu(conv)
        xs = conv[:, :inner]
        bmat = conv[:, inner : inner + state].astype(BF16)
        cmat = conv[:, inner + state :].astype(BF16)
        c_ref[b] = cmat
        dt = softplus(step_ref[b].astype(F32) + bias_ref[...])
        dt = jnp.where(line >= start_ref[b], dt, 0.0)
        cumul = jnp.dot(
            lower.astype(F32), -dt * rate_ref[...],
            precision=lax.Precision.HIGHEST, preferred_element_type=F32,
        )
        cumul_t = cumul.T
        last = cumul[rows - 1 : rows, :]
        scores = lax.dot_general(cmat, bmat, (((1,), (1,)), ((), ())), preferred_element_type=F32)
        scores = jnp.where(lower, scores, 0.0)
        drive = per_head(dt, heads, size) * xs
        drive16 = drive.astype(BF16)
        from_held = lax.dot_general(
            cmat, held[b].astype(BF16), (((1,), (1,)), ((), ())), preferred_element_type=F32
        )
        y = per_head(jnp.exp(cumul), heads, size) * from_held
        parts = []
        for h in range(heads):
            diff = cumul[:, h : h + 1] - cumul_t[h : h + 1, :]
            weighting = (jnp.exp(jnp.minimum(diff, 0.0)) * scores).astype(BF16)
            parts.append(
                jnp.dot(
                    weighting, drive16[:, h * size : (h + 1) * size], preferred_element_type=F32
                )
            )
        y_ref[b] = y + jnp.concatenate(parts, axis=1)
        to_end = per_head(jnp.exp(last - cumul), heads, size)
        added = lax.dot_general(
            (to_end * drive).astype(BF16), bmat, (((0,), (0,)), ((), ())),
            preferred_element_type=F32,
        )
        for h in range(heads):
            keep = jnp.exp(last[:, h : h + 1])
            at = slice(h * size, (h + 1) * size)
            held[b, at, :] = keep * held[b, at, :] + added[at, :]
        grow_ref[b] = jnp.exp(cumul + passed[b, 0:1, :])
        passed[b] = passed[b] + last
    sec_ref[...] = held[...]
    total_ref[...] = jnp.exp(passed[...])


def scan_section(proj, before, taps, bias, rate, start, heads, inner, state):
    batch, length = proj.shape[:2]
    mix = inner + 2 * state
    step_at = mix // LANES
    whole = lambda shape: pl.BlockSpec(shape, lambda i: (0,) * len(shape))
    rows = lambda width, at=0: pl.BlockSpec((batch, CHUNK, width), lambda i: (0, i, at))
    return pl.pallas_call(
        functools.partial(scan_kernel, heads, inner, state),
        grid=(length // CHUNK,),
        in_specs=[
            rows(mix),
            rows(LANES, step_at),
            whole((batch, 16, mix)),
            whole((CONV, mix)),
            whole((1, LANES)),
            whole((1, LANES)),
            pl.BlockSpec(memory_space=pltpu.SMEM),
        ],
        out_specs=[
            rows(inner),
            rows(state),
            rows(LANES),
            whole((batch, inner, state)),
            whole((batch, 8, LANES)),
        ],
        out_shape=[
            jax.ShapeDtypeStruct((batch, length, inner), F32),
            jax.ShapeDtypeStruct((batch, length, state), BF16),
            jax.ShapeDtypeStruct((batch, length, LANES), F32),
            jax.ShapeDtypeStruct((batch, inner, state), F32),
            jax.ShapeDtypeStruct((batch, 8, LANES), F32),
        ],
        scratch_shapes=[
            pltpu.VMEM((batch, 8, mix), F32),
            pltpu.VMEM((batch, inner, state), F32),
            pltpu.VMEM((batch, 8, LANES), F32),
        ],
        cost_estimate=pl.CostEstimate(
            flops=2 * batch * length * inner * 4 * LANES, bytes_accessed=batch * length * 4096,
            transcendentals=batch * length * 2048,
        ),
        name="section_scan",
    )(proj, proj, before, taps, bias, rate, start)


def remote(src, dst, send_sem, recv_sem, axis, index):
    return pltpu.make_async_remote_copy(
        src_ref=src, dst_ref=dst, send_sem=send_sem, recv_sem=recv_sem,
        device_id={axis: index}, device_id_type=pl.DeviceIdType.MESH,
    )


def greet(axes):
    barrier = pltpu.get_barrier_semaphore()
    count = 0
    for axis in axes:
        n = lax.axis_size(axis)
        me = lax.axis_index(axis)
        for o in range(1, n):
            pl.semaphore_signal(
                barrier, inc=1, device_id={axis: lax.rem(me + o, n)},
                device_id_type=pl.DeviceIdType.MESH,
            )
        count += n - 1
    pl.semaphore_wait(barrier, count)


def line_gather(x_ref, got, sems, recv, use, pieces, between, prepare=None):
    left_sem, right_sem, side_sem = sems
    n = lax.axis_size("head")
    chips = n // 2
    me = lax.axis_index("head")
    chip, core = me // 2, me % 2
    other = chip * 2 + 1 - core
    rows = x_ref.shape[0] // pieces

    def at(j):
        return pl.ds(pl.multiple_of(j * rows, rows), rows)

    def passed_on(src, slot, j, sem, index):
        return remote(src, got.at[slot, at(j)], sem.at[slot, j], recv.at[slot, j], "head", index)

    def arrived(slot, j):
        passed_on(got.at[slot, at(j)], slot, j, side_sem, other).wait_recv()

    def on_right(src, slot, j):
        return passed_on(src, slot, j, right_sem, me + 2)

    def on_left(src, slot, j):
        return passed_on(src, slot, j, left_sem, me - 2)

    def on_side(src, slot, j):
        return passed_on(src, slot, j, side_sem, other)

    has_right, has_left = chip + 1 < chips, chip > 0

    @pl.loop(0, pieces)
    def _(j):
        if prepare is not None:
            prepare(j, at(j))

        @pl.when(has_right)
        def _():
            on_right(x_ref.at[at(j)], me, j).start()

        @pl.when(has_left)
        def _():
            on_left(x_ref.at[at(j)], me, j).start()

        on_side(x_ref.at[at(j)], me, j).start()

    between(0)

    @pl.loop(0, pieces)
    def _(j):
        use(x_ref[at(j), :], me, at(j))

    def from_side(d, j):
        def here(q):
            slot = q * 2 + 1 - core
            arrived(slot, j)
            use(got[slot, at(j), :], slot, at(j))

        @pl.when(chip - d >= 0)
        def _():
            here(chip - d)

        @pl.when((chip + d < chips) & (d > 0))
        def _():
            here(chip + d)

    def step(t):
        d, j = t // pieces + 1, t % pieces
        low, high = (chip - d) * 2 + core, (chip + d) * 2 + core

        @pl.when(chip - d >= 0)
        def _():
            arrived(low, j)
            block = got.at[low, at(j)]

            @pl.when(has_right)
            def _():
                on_right(block, low, j).start()

            on_side(block, low, j).start()

        @pl.when(chip + d < chips)
        def _():
            arrived(high, j)
            block = got.at[high, at(j)]

            @pl.when(has_left)
            def _():
                on_left(block, high, j).start()

            on_side(block, high, j).start()

        @pl.when(chip - d >= 0)
        def _():
            use(got[low, at(j), :], low, at(j))

        @pl.when(chip + d < chips)
        def _():
            use(got[high, at(j), :], high, at(j))

        from_side(d - 1, j)

    pl.loop(0, pieces)(step)
    between(1)
    pl.loop(pieces, (chips - 1) * pieces)(step)

    @pl.loop(0, pieces)
    def _(j):
        from_side(chips - 1, j)

    @pl.loop(0, chips * pieces)
    def _(t):
        q, j = t // pieces, t % pieces
        slot = q * 2 + core
        block = got.at[slot, at(j)]
        on_side(block, slot, j).wait_send()

        @pl.when(has_right & (q <= chip))
        def _():
            on_right(block, slot, j).wait_send()

        @pl.when(has_left & (q >= chip))
        def _():
            on_left(block, slot, j).wait_send()

    between(2)


def project_kernel(
    pieces, batch, inner, x_ref, value_ref, bc_ref, step_ref, gate_w_ref, wo_ref, kept_ref,
    mixin_ref, gate_ref, cols_ref, before_ref, pool_ref,
    got, total, w, left_sem, right_sem, side_sem, recv, w_sem,
    out_send, out_recv, seq_send, seq_recv, kept_send, kept_recv, tail_send, tail_recv, own_sem,
):
    n, n_seq = lax.axis_size("head"), lax.axis_size("seq")
    me, sec = lax.axis_index("head"), lax.axis_index("seq")
    part, width = cols_ref.shape[2:]
    length = x_ref.shape[0] // batch
    mix = value_ref.shape[2] + bc_ref.shape[2]
    gate_at = mixin_ref.shape[1]
    greet(("head", "seq"))

    def weight_copies():
        copies, column = [], 0
        for i, ref in enumerate((value_ref, bc_ref, step_ref, gate_w_ref)):
            wide = ref.shape[2]
            copies.append(
                pltpu.make_async_copy(ref, w.at[:, :, column : column + wide], w_sem.at[i])
            )
            column += wide
        return copies

    def columns(to):
        return wo_ref.at[
            pl.ds(pl.multiple_of(sec * part, part), part), pl.ds(pl.multiple_of(to * width, width), width)
        ]

    def spread(o):
        to = lax.rem(me + o, n)
        return remote(columns(to), cols_ref.at[sec, me], out_send.at[o], out_recv.at[me], "head", to)

    def landed(o):
        frm = lax.rem(me + o, n)
        remote(
            columns(frm), cols_ref.at[sec, frm], out_send.at[o], out_recv.at[frm], "head", frm
        ).wait_recv()

    def shared(o):
        to = lax.rem(sec + o, n_seq)
        return remote(cols_ref.at[sec], cols_ref.at[sec], seq_send.at[o], seq_recv.at[sec], "seq", to)

    def got_share(o):
        frm = lax.rem(sec + o, n_seq)
        remote(
            cols_ref.at[frm], cols_ref.at[frm], seq_send.at[o], seq_recv.at[frm], "seq", frm
        ).wait_recv()

    def kept_to(o):
        to = lax.rem(sec + o, n_seq)
        return remote(kept_ref, pool_ref.at[sec], kept_send.at[o], kept_recv.at[sec], "seq", to)

    def kept_from(o):
        frm = lax.rem(sec + o, n_seq)
        remote(kept_ref, pool_ref.at[frm], kept_send.at[o], kept_recv.at[frm], "seq", frm).wait_recv()

    def own_cols():
        return pltpu.make_async_copy(columns(me), cols_ref.at[sec, me], own_sem.at[0])

    def own_kept():
        return pltpu.make_async_copy(kept_ref, pool_ref.at[sec], own_sem.at[1])

    def tail_copy(b, index):
        return remote(
            mixin_ref.at[pl.ds((b + 1) * length - 16, 16), pl.ds(0, mix)],
            before_ref.at[b], tail_send.at[b], tail_recv.at[b], "seq", index,
        )

    def between(stage):
        if stage == 0:
            copies = weight_copies()
            for copy in copies:
                copy.start()
            own_cols().start()
            own_kept().start()
            pl.loop(1, n)(lambda o: spread(o).start())
            pl.loop(1, n_seq)(lambda o: kept_to(o).start())
            total[...] = jnp.zeros_like(total)
            for copy in copies:
                copy.wait()
        elif stage == 1:
            own_cols().wait()
            pl.loop(1, n)(landed)
            pl.loop(1, n_seq)(lambda o: shared(o).start())
        else:
            own_kept().wait()
            pl.loop(1, n)(lambda o: spread(o).wait_send())
            pl.loop(1, n_seq)(lambda o: shared(o).wait_send())
            pl.loop(1, n_seq)(got_share)
            pl.loop(1, n_seq)(lambda o: kept_to(o).wait_send())
            pl.loop(1, n_seq)(kept_from)

    def use(block, slot, at):
        total[at, :] += jnp.dot(block, w[slot], preferred_element_type=F32)

    line_gather(x_ref, got, (left_sem, right_sem, side_sem), recv, use, pieces, between)

    for b in range(batch):
        at = pl.ds((b + 1) * length - 16, 16)
        mixin_ref[at, :] = total[at, :gate_at].astype(BF16)

        @pl.when(sec + 1 < n_seq)
        def _():
            tail_copy(b, sec + 1).start()

        @pl.when(sec == 0)
        def _():
            before_ref[b] = jnp.zeros(before_ref.shape[1:], BF16)

    rows = length // (pieces // batch)
    for b in range(batch):
        for j in range(pieces // batch):
            begin = b * length + j * rows
            gate_ref[begin : begin + rows, :] = total[begin : begin + rows, gate_at:].astype(BF16)
            end = min(begin + rows, (b + 1) * length - 16)
            mixin_ref[begin:end, :] = total[begin:end, :gate_at].astype(BF16)

    for b in range(batch):

        @pl.when(sec + 1 < n_seq)
        def _():
            tail_copy(b, sec + 1).wait_send()

        @pl.when(sec > 0)
        def _():
            tail_copy(b, sec - 1).wait_recv()


def mix_kernel(
    pieces, heads, y_ref, c_ref, grow_ref, gate_ref, sent_ref, pool_ref, gain_ref, w_ref,
    owner_ref, start_ref, out_ref, sums_ref,
    got, x, sq, states, incoming, left_sem, right_sem, side_sem, recv,
    sq_send, sq_recv, own_sem, st_send, st_recv,
):
    n, n_seq = lax.axis_size("head"), lax.axis_size("seq")
    me, sec = lax.axis_index("head"), lax.axis_index("seq")
    parts, _, part, width = w_ref.shape
    batch, inner, state = pool_ref.shape[1:]
    size = inner // heads
    rows = x.shape[0] // pieces
    length = x.shape[0] // batch
    greet(("head", "seq"))

    def state_copy(to, frm):
        return remote(sent_ref, states.at[frm], st_send.at[to], st_recv.at[frm], "seq", to)

    for r in range(n_seq):

        @pl.when(sec < r)
        def _():
            state_copy(r, sec).start()

    out_ref[...] = jnp.zeros_like(out_ref)
    for b in range(batch):
        first = owner_ref[0, b] * pool_ref[0, b].astype(F32)
        for r in range(1, n_seq):
            first = first + owner_ref[r, b] * pool_ref[r, b].astype(F32)
        incoming[b] = first

    for r in range(n_seq - 1):

        @pl.when(sec > r)
        def _():
            state_copy(sec, r).wait_recv()
            for b in range(batch):
                decay = states[r, b, inner : inner + 16, :].astype(F32)
                for h in range(heads):
                    at = slice(h * size, (h + 1) * size)
                    one = decay[0:1, h : h + 1] + decay[8:9, h : h + 1]
                    incoming[b, at, :] = one * incoming[b, at, :] + states[r, b, at, :].astype(F32)

    def prepare(j, at):
        b = j // (pieces // batch)
        carry = lax.dot_general(
            c_ref[at, :], incoming[b].astype(BF16), (((1,), (1,)), ((), ())),
            preferred_element_type=F32,
        )
        y = y_ref[at, :] + per_head(grow_ref[at, :], heads, size) * carry
        line = lax.broadcasted_iota(jnp.int32, (rows, inner), 0) + (j * rows - b * length)
        y = jnp.where(line >= start_ref[b], y, 0.0)
        gated = y * silu(gate_ref[at, :].astype(F32))
        x[at, :] = (gated * gain_ref[...]).astype(BF16)
        sq[pl.ds(j, 1), :] = lax.dot_general(
            jnp.ones((8, inner), F32), gated * gated, (((1,), (1,)), ((), ())),
            precision=lax.Precision.HIGHEST, preferred_element_type=F32,
        )[0:1, :]

    def sums_to(o):
        to = lax.rem(me + o, n)
        return remote(sq, sums_ref.at[me], sq_send.at[o], sq_recv.at[me], "head", to)

    def sums_from(o):
        frm = lax.rem(me + o, n)
        remote(sq, sums_ref.at[frm], sq_send.at[o], sq_recv.at[frm], "head", frm).wait_recv()

    def own_copy():
        return pltpu.make_async_copy(sq, sums_ref.at[me], own_sem)

    def between(stage):
        if stage == 0:
            own_copy().start()
            pl.loop(1, n)(lambda o: sums_to(o).start())
        elif stage == 2:
            own_copy().wait()
            pl.loop(1, n)(lambda o: sums_to(o).wait_send())
            pl.loop(1, n)(sums_from)

    def use(block, slot, at):
        weights = w_ref[:, slot].reshape(parts * part, width)
        out_ref[at, :] += jnp.dot(block, weights, preferred_element_type=F32)

    line_gather(x, got, (left_sem, right_sem, side_sem), recv, use, pieces, between, prepare)

    for r in range(n_seq):

        @pl.when(sec < r)
        def _():
            state_copy(r, sec).wait_send()


VMEM_SPEC = pl.BlockSpec(memory_space=pltpu.VMEM)
SMEM_SPEC = pl.BlockSpec(memory_space=pltpu.SMEM)
ANY_SPEC = pl.BlockSpec(memory_space=pl.ANY)


def gather_scratch(n, rows, width, pieces):
    sem = pltpu.SemaphoreType.DMA((n, pieces))
    return [pltpu.VMEM((n, rows, width), BF16)], [sem, sem, sem, sem]


def gather_project(x, w_value, w_bc, w_step, w_gate, w_out, kept, pieces=8):
    rows, width = x.shape
    n, n_seq = lax.axis_size("head"), lax.axis_size("seq")
    parts = [w.reshape(n, width, w.shape[1]) for w in (w_value, w_bc, w_step, w_gate)]
    wide = sum(w.shape[2] for w in parts)
    inner = w_gate.shape[1]
    mix = w_value.shape[1] + w_bc.shape[1]
    batch = kept.shape[0]
    depth, model = w_out.shape
    slots, sems = gather_scratch(n, rows, width, pieces)
    dma = pltpu.SemaphoreType.DMA
    return pl.pallas_call(
        functools.partial(project_kernel, pieces, batch, inner),
        in_specs=[VMEM_SPEC] + [ANY_SPEC] * 4 + [VMEM_SPEC] * 2,
        out_specs=[VMEM_SPEC] * 5,
        out_shape=[
            jax.ShapeDtypeStruct((rows, wide - inner), BF16),
            jax.ShapeDtypeStruct((rows, inner), BF16),
            jax.ShapeDtypeStruct((n_seq, n, depth // n_seq, model // n), BF16),
            jax.ShapeDtypeStruct((batch, 16, mix), BF16),
            jax.ShapeDtypeStruct((n_seq,) + kept.shape, BF16),
        ],
        scratch_shapes=slots
        + [pltpu.VMEM((rows, wide), F32), pltpu.VMEM((n, width, wide), BF16)]
        + sems
        + [dma((4,)), dma((n,)), dma((n,))]
        + [dma((n_seq,))] * 4
        + [dma((batch,)), dma((batch,)), dma((2,))],
        compiler_params=pltpu.CompilerParams(
            collective_id=0, has_side_effects=True, vmem_limit_bytes=56 * 2**20
        ),
        name="gather_project",
    )(x, *parts, w_out, kept)


def gather_mix(y, cmat, grow, gate, sent, pool, gain, w_cols, owner, start, heads, pieces=8):
    rows, inner = y.shape
    n, n_seq = lax.axis_size("head"), lax.axis_size("seq")
    batch, state = pool.shape[1], pool.shape[3]
    slots, sems = gather_scratch(n, rows, inner, pieces)
    dma = pltpu.SemaphoreType.DMA
    return pl.pallas_call(
        functools.partial(mix_kernel, pieces, heads),
        in_specs=[VMEM_SPEC] * 8 + [SMEM_SPEC] * 2,
        out_specs=[VMEM_SPEC] * 2,
        out_shape=[
            jax.ShapeDtypeStruct((rows, w_cols.shape[3]), F32),
            jax.ShapeDtypeStruct((n, pieces, rows // pieces), F32),
        ],
        scratch_shapes=slots
        + [
            pltpu.VMEM((rows, inner), BF16),
            pltpu.VMEM((pieces, rows // pieces), F32),
            pltpu.VMEM((n_seq,) + sent.shape, BF16),
            pltpu.VMEM((batch, inner, state), F32),
        ]
        + sems
        + [dma((n,)), dma((n,)), dma(()), dma((n_seq,)), dma((n_seq,))],
        compiler_params=pltpu.CompilerParams(
            collective_id=1, has_side_effects=True, vmem_limit_bytes=48 * 2**20
        ),
        name="gather_mix",
    )(y, cmat, grow, gate, sent, pool, gain, w_cols, owner, start)


def high_low(x):
    high = x.astype(BF16)
    return high, (x - high.astype(F32)).astype(BF16)


def per_device(
    tokens, w_gate, w_value, w_bc, w_step, step_bias, rate, conv_value, conv_bc, norm_gain,
    w_out, kept_states, kept_index, cached_len,
):
    batch, sec_len, d_part = tokens.shape
    inner = w_gate.shape[1]
    heads = w_step.shape[1]
    size = inner // heads
    state = w_bc.shape[1] // 2
    mix = inner + 2 * state
    slots = kept_states.shape[0]
    n_seq = lax.axis_size("seq")
    n_head = lax.axis_size("head")
    sec = lax.axis_index("seq")

    tokens_all = batch * sec_len
    taps = jnp.concatenate([conv_value, conv_bc], axis=1)
    bias = jnp.pad(step_bias, (0, LANES - heads))[None]
    rates = jnp.pad(rate, (0, LANES - heads))[None]
    picked = jnp.stack(
        [lax.dynamic_index_in_dim(kept_states, kept_index[b] % slots, 0, False) for b in range(batch)]
    ).astype(BF16).reshape(batch, inner, state)
    start = cached_len - sec * sec_len
    owner = (jnp.arange(n_seq)[:, None] == (kept_index // slots)[None, :]).astype(F32)

    mixin, gate, w_cols, before, pool = gather_project(
        tokens.reshape(tokens_all, d_part), w_value, w_bc,
        jnp.pad(w_step, ((0, 0), (0, LANES - heads))), w_gate, w_out, picked,
    )
    y, cmat, grow, sec_state, total = scan_section(
        mixin.reshape(batch, sec_len, -1), before, taps, bias, rates, start, heads, inner, state
    )
    high, low = high_low(total)
    sent = jnp.concatenate([sec_state.astype(BF16), high, low], axis=1)
    mixed, sums = gather_mix(
        y.reshape(tokens_all, inner), cmat.reshape(tokens_all, state),
        grow.reshape(tokens_all, LANES), gate, sent, pool, norm_gain[None], w_cols, owner, start,
        heads,
    )
    meansq = jnp.sum(sums, axis=0).reshape(-1) / (inner * n_head)
    out = (mixed * lax.rsqrt(meansq + 1e-05)[:, None]).astype(BF16)
    return out.reshape(batch, sec_len, d_part)


def solution(mesh):
    return jax.shard_map(
        per_device,
        mesh=mesh,
        in_specs=(
            P(None, "seq", "head"),
            P(None, "head"),
            P(None, "head"),
            P(),
            P(None, "head"),
            P("head"),
            P("head"),
            P(None, "head"),
            P(),
            P("head"),
            P("head", None),
            P("seq", "head", None, None),
            P(),
            P(),
        ),
        out_specs=P(None, "seq", "head"),
        check_vma=False,
    )
```

```python
import functools

import jax
import jax.numpy as jnp
from jax import lax
from jax.experimental import pallas as pl
from jax.experimental.pallas import tpu as pltpu
from jax.sharding import PartitionSpec as P

CONV = 4
LANES = 128
CHUNK = 128
F32 = jnp.float32
BF16 = jnp.bfloat16


def silu(x):
    return x * (0.5 + 0.5 * jnp.tanh(0.5 * x))


def softplus(x):
    return jnp.maximum(x, 0.0) + jnp.log1p(jnp.exp(-jnp.abs(x)))


def per_head(cols, heads, size):
    rows = cols.shape[0]
    return jnp.concatenate(
        [jnp.broadcast_to(cols[:, h : h + 1], (rows, size)) for h in range(heads)], axis=1
    )


def scan_kernel(
    heads, inner, state, mixin_ref, step_ref, before_ref, value_taps_ref, bc_taps_ref, bias_ref, rate_ref,
    cached_ref, y_ref, c_ref, grow_ref, sent_ref, tail, held, passed,
):
    i = pl.program_id(0)
    batch, rows = mixin_ref.shape[:2]
    size = inner // heads

    @pl.when(i == 0)
    def _():
        tail[...] = before_ref[:, 8:, :].astype(F32)
        held[...] = jnp.zeros_like(held)
        passed[...] = jnp.zeros_like(passed)

    tri_r = lax.broadcasted_iota(jnp.int32, (rows, rows), 0)
    tri_c = lax.broadcasted_iota(jnp.int32, (rows, rows), 1)
    lower = tri_r >= tri_c
    at_row = lax.axis_index("seq") * pl.num_programs(0) + i
    line = lax.broadcasted_iota(jnp.int32, (rows, LANES), 0) + at_row * rows
    lane = lax.broadcasted_iota(jnp.int32, (1, LANES), 1)
    bias = jnp.zeros((1, LANES), F32)
    rate = jnp.zeros((1, LANES), F32)
    for h in range(heads):
        bias = jnp.where(lane == h, bias_ref[h], bias)
        rate = jnp.where(lane == h, rate_ref[h], rate)
    taps = jnp.concatenate([value_taps_ref[...], bc_taps_ref[...]], axis=1)
    for b in range(batch):
        mixin = mixin_ref[b].astype(F32)
        padded = jnp.concatenate([tail[b], mixin], axis=0)
        tail[b] = mixin[rows - 8 :, :]
        first = 8 - CONV + 1
        conv = taps[0:1, :] * padded[first : first + rows, :]
        for k in range(1, CONV):
            conv = conv + taps[k : k + 1, :] * padded[first + k : first + k + rows, :]
        conv = silu(conv)
        xs = conv[:, :inner]
        bmat = conv[:, inner : inner + state].astype(BF16)
        cmat = conv[:, inner + state :].astype(BF16)
        c_ref[b] = cmat
        dt = softplus(step_ref[b].astype(F32) + bias)
        dt = jnp.where(line >= cached_ref[b], dt, 0.0)
        cumul = jnp.dot(
            lower.astype(F32), -dt * rate,
            precision=lax.Precision.HIGHEST, preferred_element_type=F32,
        )
        cumul_t = cumul.T
        last = cumul[rows - 1 : rows, :]
        scores = lax.dot_general(cmat, bmat, (((1,), (1,)), ((), ())), preferred_element_type=F32)
        scores = jnp.where(lower, scores, 0.0)
        drive = per_head(dt, heads, size) * xs
        drive16 = drive.astype(BF16)
        from_held = lax.dot_general(
            cmat, held[b].astype(BF16), (((1,), (1,)), ((), ())), preferred_element_type=F32
        )
        y = per_head(jnp.exp(cumul), heads, size) * from_held
        parts = []
        for h in range(heads):
            diff = cumul[:, h : h + 1] - cumul_t[h : h + 1, :]
            weighting = (jnp.exp(jnp.minimum(diff, 0.0)) * scores).astype(BF16)
            parts.append(
                jnp.dot(
                    weighting, drive16[:, h * size : (h + 1) * size], preferred_element_type=F32
                )
            )
        y_ref[b] = (y + jnp.concatenate(parts, axis=1)).astype(BF16)
        to_end = per_head(jnp.exp(last - cumul), heads, size)
        added = lax.dot_general(
            (to_end * drive).astype(BF16), bmat, (((0,), (0,)), ((), ())),
            preferred_element_type=F32,
        )
        for h in range(heads):
            keep = jnp.exp(last[:, h : h + 1])
            at = slice(h * size, (h + 1) * size)
            held[b, at, :] = keep * held[b, at, :] + added[at, :]
        grow_ref[b] = jnp.exp(cumul + passed[b, 0:1, :])
        passed[b] = passed[b] + last

    @pl.when(i == pl.num_programs(0) - 1)
    def _():
        for b in range(batch):
            high, low = high_low(jnp.exp(passed[b]))
            sent_ref[b] = jnp.concatenate([held[b].astype(BF16), high, low], axis=0)


def scan_section(proj, before, value_taps, bc_taps, bias, rate, cached, heads, inner, state):
    batch, length = proj.shape[:2]
    mix = inner + 2 * state
    step_at = mix // LANES
    whole = lambda shape: pl.BlockSpec(shape, lambda i: (0,) * len(shape))
    rows = lambda width, at=0: pl.BlockSpec((batch, CHUNK, width), lambda i: (0, i, at))
    return pl.pallas_call(
        functools.partial(scan_kernel, heads, inner, state),
        grid=(length // CHUNK,),
        in_specs=[
            rows(mix),
            rows(LANES, step_at),
            whole((batch, 16, mix)),
            whole((CONV, inner)),
            whole((CONV, 2 * state)),
            pl.BlockSpec(memory_space=pltpu.SMEM),
            pl.BlockSpec(memory_space=pltpu.SMEM),
            pl.BlockSpec(memory_space=pltpu.SMEM),
        ],
        out_specs=[
            rows(inner),
            rows(state),
            rows(LANES),
            whole((batch, inner + 16, state)),
        ],
        out_shape=[
            jax.ShapeDtypeStruct((batch, length, inner), BF16),
            jax.ShapeDtypeStruct((batch, length, state), BF16),
            jax.ShapeDtypeStruct((batch, length, LANES), F32),
            jax.ShapeDtypeStruct((batch, inner + 16, state), BF16),
        ],
        scratch_shapes=[
            pltpu.VMEM((batch, 8, mix), F32),
            pltpu.VMEM((batch, inner, state), F32),
            pltpu.VMEM((batch, 8, LANES), F32),
        ],
        cost_estimate=pl.CostEstimate(
            flops=2 * batch * length * inner * 4 * LANES, bytes_accessed=batch * length * 4096,
            transcendentals=batch * length * 2048,
        ),
        name="section_scan",
    )(proj, proj, before, value_taps, bc_taps, bias, rate, cached)


def remote(src, dst, send_sem, recv_sem, axis, index):
    return pltpu.make_async_remote_copy(
        src_ref=src, dst_ref=dst, send_sem=send_sem, recv_sem=recv_sem,
        device_id={axis: index}, device_id_type=pl.DeviceIdType.MESH,
    )


def greet(axes):
    barrier = pltpu.get_barrier_semaphore()
    count = 0
    for axis in axes:
        n = lax.axis_size(axis)
        me = lax.axis_index(axis)
        for o in range(1, n):
            pl.semaphore_signal(
                barrier, inc=1, device_id={axis: lax.rem(me + o, n)},
                device_id_type=pl.DeviceIdType.MESH,
            )
        count += n - 1
    pl.semaphore_wait(barrier, count)


def line_gather(x_ref, got, sems, recv, use, pieces, between, prepare=None):
    left_sem, right_sem, side_sem = sems
    n = lax.axis_size("head")
    chips = n // 2
    me = lax.axis_index("head")
    chip, core = me // 2, me % 2
    other = chip * 2 + 1 - core
    rows = x_ref.shape[0] // pieces

    def at(j):
        return pl.ds(pl.multiple_of(j * rows, rows), rows)

    def passed_on(src, slot, j, sem, index):
        return remote(src, got.at[slot, at(j)], sem.at[slot, j], recv.at[slot, j], "head", index)

    def arrived(slot, j):
        passed_on(got.at[slot, at(j)], slot, j, side_sem, other).wait_recv()

    def on_right(src, slot, j):
        return passed_on(src, slot, j, right_sem, me + 2)

    def on_left(src, slot, j):
        return passed_on(src, slot, j, left_sem, me - 2)

    def on_side(src, slot, j):
        return passed_on(src, slot, j, side_sem, other)

    has_right, has_left = chip + 1 < chips, chip > 0

    @pl.loop(0, pieces)
    def _(j):
        if prepare is not None:
            prepare(j, at(j))

        @pl.when(has_right)
        def _():
            on_right(x_ref.at[at(j)], me, j).start()

        @pl.when(has_left)
        def _():
            on_left(x_ref.at[at(j)], me, j).start()

        on_side(x_ref.at[at(j)], me, j).start()

    between(0)

    @pl.loop(0, pieces)
    def _(j):
        use(x_ref[at(j), :], me, at(j))

    def from_side(d, j):
        def here(q):
            slot = q * 2 + 1 - core
            arrived(slot, j)
            use(got[slot, at(j), :], slot, at(j))

        @pl.when(chip - d >= 0)
        def _():
            here(chip - d)

        @pl.when((chip + d < chips) & (d > 0))
        def _():
            here(chip + d)

    def step(t):
        d, j = t // pieces + 1, t % pieces
        low, high = (chip - d) * 2 + core, (chip + d) * 2 + core

        @pl.when(chip - d >= 0)
        def _():
            arrived(low, j)
            block = got.at[low, at(j)]

            @pl.when(has_right)
            def _():
                on_right(block, low, j).start()

            on_side(block, low, j).start()

        @pl.when(chip + d < chips)
        def _():
            arrived(high, j)
            block = got.at[high, at(j)]

            @pl.when(has_left)
            def _():
                on_left(block, high, j).start()

            on_side(block, high, j).start()

        @pl.when(chip - d >= 0)
        def _():
            use(got[low, at(j), :], low, at(j))

        @pl.when(chip + d < chips)
        def _():
            use(got[high, at(j), :], high, at(j))

        from_side(d - 1, j)

    pl.loop(0, pieces)(step)
    between(1)
    pl.loop(pieces, (chips - 1) * pieces)(step)

    @pl.loop(0, pieces)
    def _(j):
        from_side(chips - 1, j)

    @pl.loop(0, chips * pieces)
    def _(t):
        q, j = t // pieces, t % pieces
        slot = q * 2 + core
        block = got.at[slot, at(j)]
        on_side(block, slot, j).wait_send()

        @pl.when(has_right & (q <= chip))
        def _():
            on_right(block, slot, j).wait_send()

        @pl.when(has_left & (q >= chip))
        def _():
            on_left(block, slot, j).wait_send()

    between(2)


def project_kernel(
    pieces, batch, inner, x_ref, value_ref, bc_ref, step_ref, gate_w_ref, wo_ref, kept_ref,
    mixin_ref, gate_ref, cols_ref, before_ref, pool_ref,
    got, total, w, left_sem, right_sem, side_sem, recv, w_sem,
    out_send, out_recv, seq_send, seq_recv, kept_send, kept_recv, tail_send, tail_recv, own_sem,
):
    n, n_seq = lax.axis_size("head"), lax.axis_size("seq")
    me, sec = lax.axis_index("head"), lax.axis_index("seq")
    part, width = cols_ref.shape[2:]
    length = x_ref.shape[0] // batch
    mix = value_ref.shape[2] + bc_ref.shape[2]
    gate_at = mixin_ref.shape[1]
    greet(("head", "seq"))

    def weight_copies():
        copies, column = [], 0
        for i, ref in enumerate((value_ref, bc_ref, step_ref, gate_w_ref)):
            wide = ref.shape[2]
            copies.append(
                pltpu.make_async_copy(ref, w.at[:, :, column : column + wide], w_sem.at[i])
            )
            column += wide
        return copies

    def columns(to):
        return wo_ref.at[
            pl.ds(pl.multiple_of(sec * part, part), part), pl.ds(pl.multiple_of(to * width, width), width)
        ]

    def spread(o):
        to = lax.rem(me + o, n)
        return remote(columns(to), cols_ref.at[sec, me], out_send.at[o], out_recv.at[me], "head", to)

    def landed(o):
        frm = lax.rem(me + o, n)
        remote(
            columns(frm), cols_ref.at[sec, frm], out_send.at[o], out_recv.at[frm], "head", frm
        ).wait_recv()

    def shared(o):
        to = lax.rem(sec + o, n_seq)
        return remote(cols_ref.at[sec], cols_ref.at[sec], seq_send.at[o], seq_recv.at[sec], "seq", to)

    def got_share(o):
        frm = lax.rem(sec + o, n_seq)
        remote(
            cols_ref.at[frm], cols_ref.at[frm], seq_send.at[o], seq_recv.at[frm], "seq", frm
        ).wait_recv()

    def kept_to(o):
        to = lax.rem(sec + o, n_seq)
        return remote(kept_ref, pool_ref.at[sec], kept_send.at[o], kept_recv.at[sec], "seq", to)

    def kept_from(o):
        frm = lax.rem(sec + o, n_seq)
        remote(kept_ref, pool_ref.at[frm], kept_send.at[o], kept_recv.at[frm], "seq", frm).wait_recv()

    def own_cols():
        return pltpu.make_async_copy(columns(me), cols_ref.at[sec, me], own_sem.at[0])

    def own_kept():
        return pltpu.make_async_copy(kept_ref, pool_ref.at[sec], own_sem.at[1])

    def tail_copy(b, index):
        return remote(
            mixin_ref.at[pl.ds((b + 1) * length - 16, 16), pl.ds(0, mix)],
            before_ref.at[b], tail_send.at[b], tail_recv.at[b], "seq", index,
        )

    def between(stage):
        if stage == 0:
            copies = weight_copies()
            for copy in copies:
                copy.start()
            own_cols().start()
            own_kept().start()
            pl.loop(1, n)(lambda o: spread(o).start())
            pl.loop(1, n_seq)(lambda o: kept_to(o).start())
            total[...] = jnp.zeros_like(total)
            for copy in copies:
                copy.wait()
        elif stage == 1:
            own_cols().wait()
            pl.loop(1, n)(landed)
            pl.loop(1, n_seq)(lambda o: shared(o).start())
        else:
            own_kept().wait()
            pl.loop(1, n)(lambda o: spread(o).wait_send())
            pl.loop(1, n_seq)(lambda o: shared(o).wait_send())
            pl.loop(1, n_seq)(got_share)
            pl.loop(1, n_seq)(lambda o: kept_to(o).wait_send())
            pl.loop(1, n_seq)(kept_from)

    def use(block, slot, at):
        total[at, :] += jnp.dot(block, w[slot], preferred_element_type=F32)

    line_gather(x_ref, got, (left_sem, right_sem, side_sem), recv, use, pieces, between)

    for b in range(batch):
        at = pl.ds((b + 1) * length - 16, 16)
        mixin_ref[at, :] = total[at, :gate_at].astype(BF16)

        @pl.when(sec + 1 < n_seq)
        def _():
            tail_copy(b, sec + 1).start()

        @pl.when(sec == 0)
        def _():
            before_ref[b] = jnp.zeros(before_ref.shape[1:], BF16)

    rows = length // (pieces // batch)
    for b in range(batch):
        for j in range(pieces // batch):
            begin = b * length + j * rows
            gate_ref[begin : begin + rows, :] = total[begin : begin + rows, gate_at:].astype(BF16)
            end = min(begin + rows, (b + 1) * length - 16)
            mixin_ref[begin:end, :] = total[begin:end, :gate_at].astype(BF16)

    for b in range(batch):

        @pl.when(sec + 1 < n_seq)
        def _():
            tail_copy(b, sec + 1).wait_send()

        @pl.when(sec > 0)
        def _():
            tail_copy(b, sec - 1).wait_recv()


def mix_kernel(
    pieces, heads, y_ref, c_ref, grow_ref, gate_ref, sent_ref, pool_ref, gain_ref, w_ref,
    owner_ref, cached_ref, out_ref, sums_ref,
    got, x, sq, states, incoming, left_sem, right_sem, side_sem, recv,
    sq_send, sq_recv, own_sem, st_send, st_recv,
):
    n, n_seq = lax.axis_size("head"), lax.axis_size("seq")
    me, sec = lax.axis_index("head"), lax.axis_index("seq")
    parts, _, part, width = w_ref.shape
    batch, inner, state = pool_ref.shape[1:]
    size = inner // heads
    rows = x.shape[0] // pieces
    length = x.shape[0] // batch
    greet(("head", "seq"))

    def state_copy(to, frm):
        return remote(sent_ref, states.at[frm], st_send.at[to], st_recv.at[frm], "seq", to)

    for r in range(n_seq):

        @pl.when(sec < r)
        def _():
            state_copy(r, sec).start()

    out_ref[...] = jnp.zeros_like(out_ref)
    for b in range(batch):
        first = owner_ref[0, b] * pool_ref[0, b].astype(F32)
        for r in range(1, n_seq):
            first = first + owner_ref[r, b] * pool_ref[r, b].astype(F32)
        incoming[b] = first

    for r in range(n_seq - 1):

        @pl.when(sec > r)
        def _():
            state_copy(sec, r).wait_recv()
            for b in range(batch):
                decay = states[r, b, inner : inner + 16, :].astype(F32)
                for h in range(heads):
                    at = slice(h * size, (h + 1) * size)
                    one = decay[0:1, h : h + 1] + decay[8:9, h : h + 1]
                    incoming[b, at, :] = one * incoming[b, at, :] + states[r, b, at, :].astype(F32)

    def prepare(j, at):
        b = j // (pieces // batch)
        carry = lax.dot_general(
            c_ref[at, :], incoming[b].astype(BF16), (((1,), (1,)), ((), ())),
            preferred_element_type=F32,
        )
        y = y_ref[at, :].astype(F32) + per_head(grow_ref[at, :], heads, size) * carry
        line = lax.broadcasted_iota(jnp.int32, (rows, inner), 0) + (sec * length + j * rows - b * length)
        y = jnp.where(line >= cached_ref[b], y, 0.0)
        gated = y * silu(gate_ref[at, :].astype(F32))
        x[at, :] = (gated * gain_ref[...]).astype(BF16)
        sq[pl.ds(j, 1), :] = lax.dot_general(
            jnp.ones((8, inner), F32), gated * gated, (((1,), (1,)), ((), ())),
            precision=lax.Precision.HIGHEST, preferred_element_type=F32,
        )[0:1, :]

    def sums_to(o):
        to = lax.rem(me + o, n)
        return remote(sq, sums_ref.at[me], sq_send.at[o], sq_recv.at[me], "head", to)

    def sums_from(o):
        frm = lax.rem(me + o, n)
        remote(sq, sums_ref.at[frm], sq_send.at[o], sq_recv.at[frm], "head", frm).wait_recv()

    def own_copy():
        return pltpu.make_async_copy(sq, sums_ref.at[me], own_sem)

    def between(stage):
        if stage == 0:
            own_copy().start()
            pl.loop(1, n)(lambda o: sums_to(o).start())
        elif stage == 2:
            own_copy().wait()
            pl.loop(1, n)(lambda o: sums_to(o).wait_send())
            pl.loop(1, n)(sums_from)

    def use(block, slot, at):
        weights = w_ref[:, slot].reshape(parts * part, width)
        out_ref[at, :] += jnp.dot(block, weights, preferred_element_type=F32)

    line_gather(x, got, (left_sem, right_sem, side_sem), recv, use, pieces, between, prepare)

    for r in range(n_seq):

        @pl.when(sec < r)
        def _():
            state_copy(r, sec).wait_send()


VMEM_SPEC = pl.BlockSpec(memory_space=pltpu.VMEM)
SMEM_SPEC = pl.BlockSpec(memory_space=pltpu.SMEM)
ANY_SPEC = pl.BlockSpec(memory_space=pl.ANY)


def gather_scratch(n, rows, width, pieces):
    sem = pltpu.SemaphoreType.DMA((n, pieces))
    return [pltpu.VMEM((n, rows, width), BF16)], [sem, sem, sem, sem]


def gather_project(x, w_value, w_bc, w_step, w_gate, w_out, kept, pieces=8):
    rows, width = x.shape
    n, n_seq = lax.axis_size("head"), lax.axis_size("seq")
    parts = [w.reshape(n, width, w.shape[1]) for w in (w_value, w_bc, w_step, w_gate)]
    wide = sum(w.shape[2] for w in parts)
    inner = w_gate.shape[1]
    mix = w_value.shape[1] + w_bc.shape[1]
    batch = kept.shape[0]
    depth, model = w_out.shape
    slots, sems = gather_scratch(n, rows, width, pieces)
    dma = pltpu.SemaphoreType.DMA
    return pl.pallas_call(
        functools.partial(project_kernel, pieces, batch, inner),
        in_specs=[VMEM_SPEC] + [ANY_SPEC] * 4 + [VMEM_SPEC] * 2,
        out_specs=[VMEM_SPEC] * 5,
        out_shape=[
            jax.ShapeDtypeStruct((rows, wide - inner), BF16),
            jax.ShapeDtypeStruct((rows, inner), BF16),
            jax.ShapeDtypeStruct((n_seq, n, depth // n_seq, model // n), BF16),
            jax.ShapeDtypeStruct((batch, 16, mix), BF16),
            jax.ShapeDtypeStruct((n_seq,) + kept.shape, BF16),
        ],
        scratch_shapes=slots
        + [pltpu.VMEM((rows, wide), F32), pltpu.VMEM((n, width, wide), BF16)]
        + sems
        + [dma((4,)), dma((n,)), dma((n,))]
        + [dma((n_seq,))] * 4
        + [dma((batch,)), dma((batch,)), dma((2,))],
        compiler_params=pltpu.CompilerParams(
            collective_id=0, has_side_effects=True, vmem_limit_bytes=56 * 2**20
        ),
        name="gather_project",
    )(x, *parts, w_out, kept)


def gather_mix(y, cmat, grow, gate, sent, pool, gain, w_cols, owner, start, heads, pieces=8):
    rows, inner = y.shape
    n, n_seq = lax.axis_size("head"), lax.axis_size("seq")
    batch, state = pool.shape[1], pool.shape[3]
    slots, sems = gather_scratch(n, rows, inner, pieces)
    dma = pltpu.SemaphoreType.DMA
    return pl.pallas_call(
        functools.partial(mix_kernel, pieces, heads),
        in_specs=[VMEM_SPEC] * 8 + [SMEM_SPEC] * 2,
        out_specs=[VMEM_SPEC] * 2,
        out_shape=[
            jax.ShapeDtypeStruct((rows, w_cols.shape[3]), F32),
            jax.ShapeDtypeStruct((n, pieces, rows // pieces), F32),
        ],
        scratch_shapes=slots
        + [
            pltpu.VMEM((rows, inner), BF16),
            pltpu.VMEM((pieces, rows // pieces), F32),
            pltpu.VMEM((n_seq,) + sent.shape, BF16),
            pltpu.VMEM((batch, inner, state), F32),
        ]
        + sems
        + [dma((n,)), dma((n,)), dma(()), dma((n_seq,)), dma((n_seq,))],
        compiler_params=pltpu.CompilerParams(
            collective_id=1, has_side_effects=True, vmem_limit_bytes=48 * 2**20
        ),
        name="gather_mix",
    )(y, cmat, grow, gate, sent, pool, gain, w_cols, owner, start)


def high_low(x):
    high = x.astype(BF16)
    return high, (x - high.astype(F32)).astype(BF16)


def per_device(
    tokens, w_gate, w_value, w_bc, w_step, step_bias, rate, conv_value, conv_bc, norm_gain,
    w_out, kept_states, kept_index, cached_len,
):
    batch, sec_len, d_part = tokens.shape
    inner = w_gate.shape[1]
    heads = w_step.shape[1]
    size = inner // heads
    state = w_bc.shape[1] // 2
    mix = inner + 2 * state
    slots = kept_states.shape[0]
    n_seq = lax.axis_size("seq")
    n_head = lax.axis_size("head")
    tokens_all = batch * sec_len
    picked = jnp.stack(
        [lax.dynamic_index_in_dim(kept_states, kept_index[b] % slots, 0, False) for b in range(batch)]
    ).astype(BF16).reshape(batch, inner, state)
    owner = (jnp.arange(n_seq)[:, None] == (kept_index // slots)[None, :]).astype(F32)

    mixin, gate, w_cols, before, pool = gather_project(
        tokens.reshape(tokens_all, d_part), w_value, w_bc,
        jnp.pad(w_step, ((0, 0), (0, LANES - heads))), w_gate, w_out, picked,
    )
    y, cmat, grow, sent = scan_section(
        mixin.reshape(batch, sec_len, -1), before, conv_value, conv_bc, step_bias, rate, cached_len,
        heads, inner, state,
    )
    mixed, sums = gather_mix(
        y.reshape(tokens_all, inner), cmat.reshape(tokens_all, state),
        grow.reshape(tokens_all, LANES), gate, sent, pool, norm_gain[None], w_cols, owner, cached_len,
        heads,
    )
    meansq = jnp.sum(sums, axis=0).reshape(-1) / (inner * n_head)
    out = (mixed * lax.rsqrt(meansq + 1e-05)[:, None]).astype(BF16)
    return out.reshape(batch, sec_len, d_part)


def solution(mesh):
    return jax.shard_map(
        per_device,
        mesh=mesh,
        in_specs=(
            P(None, "seq", "head"),
            P(None, "head"),
            P(None, "head"),
            P(),
            P(None, "head"),
            P("head"),
            P("head"),
            P(None, "head"),
            P(),
            P("head"),
            P("head", None),
            P("seq", "head", None, None),
            P(),
            P(),
        ),
        out_specs=P(None, "seq", "head"),
        check_vma=False,
    )
```
